128 devices in a mesh: clu: 16 (over x, z), tile: 8 (over y, core).
Axes of the slice: x: 4, y: 4, z: 4, core: 2. Of those that a mesh axis runs over, the one named last changes fastest.
Arguments:
- embeddings: bfloat16 [163840, 768], P(('clu', 'tile')), may hold values from -32 to 32
- cluster: int32 [163840], P(('clu', 'tile')), may hold values from 0 to 127, as said below
- owner_map: int32 [128], replicated, may hold values from 0 to 15, as said below
Outputs:
- best_match: float32 [163840], P(('clu', 'tile'))
The draws below stay inside these ranges and needn't reach their ends.
Inputs may be any that keep to these rules, and one draw needn't show every extreme that they name: `cluster`: among the 1280 rows of each device (aligned blocks of 1280 rows), the clusters owned by each owner (through owner_map) are named exactly 1280 / 16 times. `owner_map`: each owner index is named by exactly 8 clusters.
All inputs are finite; a program needn't handle non-finite values.
Results may differ from the reference program's by a relative error of at most 0.00077.
Values may be sent and summed in bfloat16 or wider, within the bound.
A program may use at most 192 MiB of HBM per device.

```python
import jax
import jax.numpy as jnp
from jax import lax

D = 768
R_DEV = 1280
CPO = 8
CLUSTERS = 128
ROWS = 163840
N_CLU = 16
N_TILE = 8


def owner_perm(key):
    return jax.random.permutation(key, CLUSTERS).astype(jnp.int32)


def cluster_ids(key):
    shuffled = owner_perm(key)
    inverse = jnp.argsort(shuffled).astype(jnp.int32)
    key = jax.random.fold_in(key, 7)
    key_owner, key_local = jax.random.split(key)
    pattern = (jnp.arange(R_DEV, dtype=jnp.int32) % N_CLU).astype(jnp.int32)
    device_keys = jax.random.split(key_owner, N_CLU * N_TILE)
    owners = jax.vmap(lambda sub: jax.random.permutation(sub, pattern))(device_keys).reshape(ROWS)
    level = jax.random.randint(key_local, (ROWS,), 0, 256)
    local = jnp.zeros((ROWS,), jnp.int32)
    for shift_bit in range(1, CPO):
        local = local + (level < 256 >> shift_bit).astype(jnp.int32)
    return inverse[owners * CPO + local].astype(jnp.int32)


def draw_owner_map(key, part):
    shuffled = owner_perm(key)
    return (shuffled // CPO).astype(jnp.int32)


def draw_cluster(key, part):
    return cluster_ids(key)


def draw_embeddings(key, part):
    labels = cluster_ids(key)
    key = jax.random.fold_in(key, 11)
    key_noise, key_pick, key_jitter = jax.random.split(key, 3)
    noise = jax.random.normal(key_noise, (ROWS, D), jnp.float32)
    places = jnp.arange(ROWS, dtype=jnp.int32)
    onehot = labels[:, None] == jnp.arange(CLUSTERS, dtype=jnp.int32)[None, :]
    seen = lax.cummax(jnp.where(onehot, places[:, None], jnp.int32(-1)), axis=0)
    before = jnp.concatenate([jnp.full((1, CLUSTERS), -1, jnp.int32), seen[:-1]], axis=0)
    previous = jnp.take_along_axis(before, labels[:, None], axis=1)[:, 0]
    picked = jax.random.randint(key_pick, (ROWS,), 0, 32) == 0
    source = jnp.maximum(previous, 0)
    copies = picked & (previous >= 0) & jnp.logical_not(picked[source])
    jitter = jax.random.normal(key_jitter, (ROWS, D), jnp.float32)
    copied = noise[source] + 0.05 * jitter
    rows = jnp.where(copies[:, None], copied, noise)
    return jnp.clip(rows, -8.0, 8.0).astype(jnp.bfloat16)


def setup_inputs(seed: int = 0) -> dict:
    splits = jax.random.split(jax.random.key(seed), 4)
    return {
        "embeddings": draw_embeddings(jax.random.fold_in(splits[3], 71), 0),
        "cluster": draw_cluster(jax.random.fold_in(splits[3], 71), 0),
        "owner_map": draw_owner_map(jax.random.fold_in(splits[3], 71), 0),
    }


def reference(embeddings, cluster, owner_map):
    values = embeddings.astype(jnp.float32)
    unit = (values * lax.rsqrt(lax.optimization_barrier(jnp.sum(values * values, axis=1, keepdims=True)) + 1e-06)).astype(jnp.bfloat16)
    owner = owner_map[cluster]
    order = jnp.argsort(owner, stable=True).astype(jnp.int32)
    rows_owner = ROWS // N_CLU
    grouped = order.reshape(N_CLU, rows_owner)

    def per_owner(indices):
        members = unit[indices]
        member_clu = cluster[indices]

        def per_block(query):
            q_unit = unit[query]
            q_clu = cluster[query]
            scores = jnp.dot(q_unit, members.T, preferred_element_type=jnp.float32)
            allowed = (q_clu[:, None] == member_clu[None, :]) & (query[:, None] > indices[None, :])
            return lax.optimization_barrier(jnp.max(jnp.where(allowed, scores, jnp.float32(-1.0)), axis=1))
        return lax.map(per_block, indices.reshape(rows_owner // R_DEV, R_DEV)).reshape(rows_owner)
    results = lax.map(per_owner, grouped).reshape(ROWS)
    return jnp.zeros((ROWS,), jnp.float32).at[order].set(results)
```

```python
import functools

import jax
import jax.numpy as jnp
from jax import lax
from jax.experimental import pallas as pl
from jax.experimental.pallas import tpu as pltpu
from jax.sharding import PartitionSpec as P

MESH = pl.DeviceIdType.MESH
F32 = jnp.float32
BF16 = jnp.bfloat16

SIDE = 4
OFFS = [(dx, dz) for dx in range(SIDE) for dz in range(SIDE)]
N_OWN = len(OFFS)
ROWS = 1280
SHARE = ROWS // N_OWN
WIDTH = 768
STAGES = [4, 4, 4, 4]

PAIRS = [(0, 0), (0, 1), (0, 3), (0, 2), (1, 3), (1, 2), (2, 3), (2, 4)]


def dot_t(a, b):
    return lax.dot_general(a, b, (((1,), (1,)), ((), ())), preferred_element_type=F32)


def dot(a, b):
    return jnp.dot(a, b, preferred_element_type=F32)


def split3(v):
    hi = v.astype(BF16)
    rest = v - hi.astype(F32)
    mid = rest.astype(BF16)
    low = (rest - mid.astype(F32)).astype(BF16)
    return jnp.concatenate([hi, mid, low], axis=0)


def iota(shape, dim):
    return lax.broadcasted_iota(jnp.int32, shape, dim)


def onehot(mask):
    return jnp.where(mask, F32(1.0), F32(0.0)).astype(BF16)


def kernel(
    emb, clu, omap, out,
    unit, outbox, held, msend, meta, onehot_rank, own_mask,
    lane_clu, col_info, rowacc, colacc, resend, reget, retsend, retget,
    a_s, a_r, m_s, m_r, f_s, f_r, g_s, g_r, s_s, s_r, q_s, q_r, t_s, t_r,
):
    c = lax.axis_index("clu")
    t = lax.axis_index("tile")
    x, z, y, k = c // SIDE, c % SIDE, t // 2, t % 2

    def shifted(dx, dz):
        return ((x + dx) % SIDE) * SIDE + (z + dz) % SIDE

    dest = [shifted(dx, dz) for dx, dz in OFFS]
    origin = [shifted(SIDE - dx, SIDE - dz) for dx, dz in OFFS]
    up, down = (y + 1) % SIDE, (y + SIDE - 1) % SIDE
    sib = (c, 2 * y + (1 - k))
    above, below = (c, 2 * up + k), (c, 2 * down + k)
    above_x, below_x = (c, 2 * up + (1 - k)), (c, 2 * down + (1 - k))

    barrier = pltpu.get_barrier_semaphore()
    peers = [(d, t) for d in dest[1:]] + [sib, above, below, above_x, below_x]
    for peer in peers:
        pl.semaphore_signal(barrier, inc=1, device_id=peer, device_id_type=MESH)

    def copy(src, dst, ssem, rsem, device):
        return pltpu.make_async_remote_copy(
            src_ref=src, dst_ref=dst, send_sem=ssem, recv_sem=rsem,
            device_id=device, device_id_type=MESH,
        )

    def block(j, n=1):
        return pl.ds(j * SHARE, n * SHARE)

    def normalise(i, carry):
        rows = pl.ds(i * SHARE, SHARE)
        v = emb[rows, :].astype(F32)
        unit[rows, :] = (v * lax.rsqrt(jnp.sum(v * v, axis=1, keepdims=True) + 1e-06)).astype(BF16)
        return carry

    lax.fori_loop(0, N_OWN, normalise, 0)

    ids = clu[...]
    which = onehot(iota((omap.shape[1], ROWS), 0) == ids)
    step = iota((N_OWN, omap.shape[1]), 0)
    owner_of = jnp.zeros((N_OWN, omap.shape[1]), jnp.int32)
    for j in range(N_OWN):
        owner_of = jnp.where(step == j, dest[j], owner_of)
    mine = dot(onehot(owner_of == omap[...]), which)
    own_mask[...] = mine
    part = 256
    before = onehot(iota((part, part), 0) < iota((part, part), 1))
    base = jnp.zeros((N_OWN, 1), F32)
    pieces = []
    for i in range(ROWS // part):
        piece = mine[:, i * part:(i + 1) * part]
        pieces.append(dot(piece.astype(BF16), before) + base)
        base = base + jnp.sum(piece, axis=1, keepdims=True)
    rank = jnp.sum(mine * jnp.concatenate(pieces, axis=1), axis=0, keepdims=True)
    slot = jnp.sum(mine * iota((N_OWN, ROWS), 0).astype(F32), axis=0, keepdims=True) * SHARE + rank
    slot = slot.astype(jnp.int32)
    at_rank = onehot(iota((128, ROWS), 0) == rank.astype(jnp.int32))
    onehot_rank[...] = at_rank
    labels = dot_t((mine * ids.astype(F32)).astype(BF16), at_rank)
    for j in range(N_OWN):
        msend[j] = jnp.broadcast_to(labels[j:j + 1, :], (8, 128))
    meta[0, 0] = msend[0]

    pl.semaphore_wait(barrier, len(peers))

    meta_out = []
    for j in range(1, N_OWN):
        meta_out.append(copy(msend.at[j], meta.at[0, j], m_s.at[j], m_r.at[j], (dest[j], t)))
        meta_out[-1].start()

    def forward(j):
        n = pl.ds(j * SHARE, SHARE)
        return [
            copy(held.at[0, n], held.at[b, n], f_s.at[b, j], f_r.at[b, j], device)
            for b, device in ((2, above), (3, below), (1, sib))
        ]

    forwards = []
    out_copies = []
    first = 0
    for n in STAGES:
        size = n * SHARE
        take = onehot(iota((size, ROWS), 0) + first * SHARE == slot)
        outbox[block(first, n), :] = dot(take, unit[...]).astype(BF16)
        for j in range(first, first + n):
            if j == 0:
                held[0, block(0), :] = outbox[block(0), :]
                forwards.append(forward(0))
                for cp in forwards[0]:
                    cp.start()
            else:
                cp = copy(
                    outbox.at[block(j)], held.at[0, block(j)], a_s.at[j], a_r.at[j], (dest[j], t)
                )
                cp.start()
                out_copies.append(cp)
        first += n

    position = iota((1, ROWS), 1)
    lane_j = position // SHARE
    lane_k = position - lane_j * SHARE
    lane_key = lane_k
    for j in range(N_OWN):
        lane_key = lane_key + jnp.where(lane_j == j, origin[j] * 1024, 0)
    lane_key = lane_key.astype(F32)
    tile_of = [t, 2 * y + (1 - k), 2 * down + k, 2 * up + k, 2 * up + (1 - k)]
    spread = onehot(iota((128, ROWS), 0) == lane_k)
    in_block = onehot(iota((N_OWN, ROWS), 0) == lane_j).astype(F32)

    for b in range(3):
        rowacc[b] = jnp.full((ROWS, 128), -1.0, F32)
    for b in range(5):
        colacc[b] = jnp.full((1, ROWS), -1.0, F32)

    def wait_own(j):
        out_copies[j - 1].wait_recv()
        forwards.append(forward(j))
        for cp in forwards[j]:
            cp.start()

    for cp in meta_out:
        cp.wait()
    meta_fwd = [
        copy(meta.at[0], meta.at[b], g_s.at[b], g_r.at[b], device)
        for b, device in ((1, sib), (2, above), (3, below), (4, below_x))
    ]
    for cp in meta_fwd:
        cp.start()

    for j in range(1, STAGES[0]):
        wait_own(j)

    for cp in meta_fwd:
        cp.wait()
    for b in range(5):
        lane = jnp.sum(in_block * dot(meta[b, :, 0, :].astype(BF16), spread), axis=0, keepdims=True)
        lane_clu[b] = lane
        if b < 3:
            key = lane_key + (tile_of[b] * 128).astype(F32)
            both = jnp.where(iota((128, ROWS), 0) == 0, lane, key)
            col_info[b] = both.T

    second = []

    def stage(first, n):
        new = block(first, n)
        size = n * SHARE
        seen = (first + n) * SHARE
        for j in range(first, first + n):
            for cp in forwards[j]:
                cp.wait_recv()
            cp = copy(
                held.at[3, block(j)], held.at[4, block(j)], s_s.at[j], s_r.at[j], sib
            )
            cp.start()
            second.append(cp)
        for a, b in PAIRS:
            if b == 4:
                for j in range(first, first + n):
                    second[j].wait_recv()
            scores = dot_t(held[a, new, :], held[b, :seen, :])
            row_clu = col_info[a, new, 0:1]
            row_key = col_info[a, new, 1:2]
            col_clu = lane_clu[b, :, :seen]
            col_key = lane_key[:, :seen] + (tile_of[b] * 128).astype(F32)
            same = jnp.where(row_clu == col_clu, scores, F32(-1.0))
            as_row = jnp.where(row_key > col_key, same, F32(-1.0))
            as_col = jnp.where(row_key < col_key, same, F32(-1.0))
            rowacc[a, new, 0:1] = jnp.maximum(
                rowacc[a, new, 0:1], jnp.max(as_row, axis=1, keepdims=True)
            )
            colacc[b, :, :seen] = jnp.maximum(
                colacc[b, :, :seen], jnp.max(as_col, axis=0, keepdims=True)
            )

    first = STAGES[0]
    done = 0
    for i in range(len(STAGES)):
        if i + 1 < len(STAGES):
            for j in range(first, first + STAGES[i + 1]):
                wait_own(j)
            first += STAGES[i + 1]
        stage(done, STAGES[i])
        done += STAGES[i]

    lanes = iota((ROWS, 128), 1)
    rows_all = jnp.where(
        lanes == 0, rowacc[0, :, 0:1], jnp.where(lanes == 1, rowacc[1, :, 0:1], rowacc[2, :, 0:1])
    ).T
    for b in range(5):
        best = colacc[b]
        if b < 3:
            best = jnp.maximum(best, rows_all[b:b + 1, :])
        resend[b] = jnp.broadcast_to(best, (8, ROWS))
    back = [
        copy(resend.at[b], reget.at[b - 1], q_s.at[b], q_r.at[b], device)
        for b, device in ((1, sib), (2, below), (3, above), (4, above_x))
    ]
    for cp in back:
        cp.start()
    for cp in back:
        cp.wait_recv()
    total = resend[0]
    for b in range(4):
        total = jnp.maximum(total, reget[b])
    parts = dot_t(split3(in_block * total[0:1, :]), spread)
    parts = parts[:N_OWN] + parts[N_OWN:2 * N_OWN] + parts[2 * N_OWN:]
    for j in range(N_OWN):
        retsend[j] = jnp.broadcast_to(parts[j:j + 1, :], (8, 128))
    retget[0] = retsend[0]
    returns = [
        copy(retsend.at[j], retget.at[j], t_s.at[j], t_r.at[j], (origin[j], t))
        for j in range(1, N_OWN)
    ]
    for cp in returns:
        cp.start()
    for cp in returns:
        cp.wait_recv()
    values = dot(split3(retget[:, 0, :]), onehot_rank[...])
    values = values[:N_OWN] + values[N_OWN:2 * N_OWN] + values[2 * N_OWN:]
    out[...] = jnp.sum(values * own_mask[...], axis=0, keepdims=True)

    for cp in out_copies + second + back + returns:
        cp.wait_send()
    for group in forwards:
        for cp in group:
            cp.wait_send()


def on_device(embeddings, cluster, owner_map):
    dma = pltpu.SemaphoreType.DMA
    scratch = [
        pltpu.VMEM((ROWS, WIDTH), BF16),
        pltpu.VMEM((ROWS, WIDTH), BF16),
        pltpu.VMEM((5, ROWS, WIDTH), BF16),
        pltpu.VMEM((N_OWN, 8, 128), F32),
        pltpu.VMEM((5, N_OWN, 8, 128), F32),
        pltpu.VMEM((128, ROWS), BF16),
        pltpu.VMEM((N_OWN, ROWS), F32),
        pltpu.VMEM((5, 1, ROWS), F32),
        pltpu.VMEM((3, ROWS, 128), F32),
        pltpu.VMEM((3, ROWS, 128), F32),
        pltpu.VMEM((5, 1, ROWS), F32),
        pltpu.VMEM((5, 8, ROWS), F32),
        pltpu.VMEM((4, 8, ROWS), F32),
        pltpu.VMEM((N_OWN, 8, 128), F32),
        pltpu.VMEM((N_OWN, 8, 128), F32),
        dma((N_OWN,)), dma((N_OWN,)),
        dma((N_OWN,)), dma((N_OWN,)),
        dma((4, N_OWN)), dma((4, N_OWN)),
        dma((5,)), dma((5,)),
        dma((N_OWN,)), dma((N_OWN,)),
        dma((5,)), dma((5,)),
        dma((N_OWN,)), dma((N_OWN,)),
    ]
    vmem = pl.BlockSpec(memory_space=pltpu.VMEM)
    best = pl.pallas_call(
        kernel,
        out_shape=jax.ShapeDtypeStruct((1, ROWS), F32),
        in_specs=[vmem, vmem, vmem],
        out_specs=vmem,
        scratch_shapes=scratch,
        compiler_params=pltpu.CompilerParams(
            collective_id=0, has_side_effects=True, vmem_limit_bytes=56 << 20
        ),
    )(embeddings, cluster.reshape(1, -1), owner_map.reshape(1, -1))
    return best.reshape(-1)


def solution(mesh):
    placed = (P(("clu", "tile"), None), P(("clu", "tile")), P())
    return jax.shard_map(
        on_device, mesh=mesh, in_specs=placed, out_specs=P(("clu", "tile")), check_vma=False
    )
```

```python
import functools

import jax
import jax.numpy as jnp
from jax import lax
from jax.experimental import pallas as pl
from jax.experimental.pallas import tpu as pltpu
from jax.sharding import PartitionSpec as P

MESH = pl.DeviceIdType.MESH
F32 = jnp.float32
BF16 = jnp.bfloat16

SIDE = 4
OFFS = [
    (0, 0),
    (0, 1), (1, 0), (0, 3), (3, 0),
    (1, 1), (3, 3), (1, 3), (3, 1),
    (0, 2), (2, 0), (1, 2), (2, 1),
    (3, 2), (2, 3), (2, 2),
]
N_OWN = len(OFFS)
ROWS = 1280
SHARE = ROWS // N_OWN
WIDTH = 768
GROUPS = [(0, 5), (5, 9), (9, 13), (13, 16)]
STAGES = [(0, 4), (4, 7), (7, 10), (10, 13), (13, 16)]
STRIP = 352
LAG = 3
ORDER = [
    "P0", "S0", "F0", "P1", "S1", "P2", "L", "W1", "F1", "W2", "F2", "S2", "M", "P3", "W3",
    "F3", "W4", "F4", "S3", "O0", "W5", "F5", "W6", "W7", "F6", "O1", "W8", "F7", "A0", "D0",
    "W9", "F8", "X0", "W10", "W11", "F9", "O2", "W12", "F10", "A1", "D1", "W13", "F11", "X1",
    "W14", "W15", "F12", "O3", "O4", "F13", "A2", "D2", "U0", "F14", "X2", "U1", "U2", "F15",
    "A3", "U3", "D3", "X3", "A4", "U4", "D4", "X4",
]


def align(n, m):
    return -(-n // m) * m


STARTS = [0]
for lo, hi in STAGES:
    STARTS.append(STARTS[-1] + align((hi - lo) * SHARE, 128))
TALL = STARTS[-1]
PLACE = [STARTS[s] + (j - lo) * SHARE for s, (lo, hi) in enumerate(STAGES) for j in range(lo, hi)]


def dot_t(a, b):
    return lax.dot_general(a, b, (((1,), (1,)), ((), ())), preferred_element_type=F32)


def dot(a, b):
    return jnp.dot(a, b, preferred_element_type=F32)


def split3(v):
    hi = v.astype(BF16)
    rest = v - hi.astype(F32)
    mid = rest.astype(BF16)
    low = (rest - mid.astype(F32)).astype(BF16)
    return jnp.concatenate([hi, mid, low], axis=0)


def iota(shape, dim):
    return lax.broadcasted_iota(jnp.int32, shape, dim)


def onehot(mask):
    return jnp.where(mask, F32(1.0), F32(0.0)).astype(BF16)


def kernel(
    emb_hbm, clu, omap, out,
    emb, unit, outbox, held, msend, meta, onehot_rank, own_mask,
    lane_clu, lane_keys, col_info, rowacc, lanebest, resend, reget, retsend, retget,
    a_s, a_r, m_s, m_r, f_s, f_r, g_s, g_r, s_s, s_r, q_s, q_r, t_s, t_r, e_s,
):
    c = lax.axis_index("clu")
    t = lax.axis_index("tile")
    x, z, y, k = c // SIDE, c % SIDE, t // 2, t % 2

    def shifted(dx, dz):
        return ((x + dx) % SIDE) * SIDE + (z + dz) % SIDE

    dest = [shifted(dx, dz) for dx, dz in OFFS]
    origin = [shifted(SIDE - dx, SIDE - dz) for dx, dz in OFFS]
    up, down = (y + 1) % SIDE, (y + SIDE - 1) % SIDE
    sib = (c, 2 * y + (1 - k))
    above, below = (c, 2 * up + k), (c, 2 * down + k)
    above_x, below_x = (c, 2 * up + (1 - k)), (c, 2 * down + (1 - k))

    load = pltpu.make_async_copy(emb_hbm, emb, e_s)
    load.start()
    barrier = pltpu.get_barrier_semaphore()
    peers = [(d, t) for d in dest[1:]] + [sib, above, below, above_x, below_x]
    for peer in peers:
        pl.semaphore_signal(barrier, inc=1, device_id=peer, device_id_type=MESH)

    def copy(src, dst, ssem, rsem, device):
        return pltpu.make_async_remote_copy(
            src_ref=src, dst_ref=dst, send_sem=ssem, recv_sem=rsem,
            device_id=device, device_id_type=MESH,
        )

    def block(j, n=1):
        return pl.ds(j * SHARE, n * SHARE)

    def place(j):
        return pl.ds(PLACE[j], SHARE)

    load.wait()
    def normalise(i, carry):
        rows = pl.ds(i * SHARE, SHARE)
        v = emb[rows, :].astype(F32)
        unit[rows, :] = (v * lax.rsqrt(jnp.sum(v * v, axis=1, keepdims=True) + 1e-06)).astype(BF16)
        return carry

    lax.fori_loop(0, N_OWN, normalise, 0)

    for s, (lo, hi) in enumerate(STAGES):
        full = STARTS[s] + (hi - lo) * SHARE
        if STARTS[s + 1] > full:
            for b in range(5):
                held[b, full:STARTS[s + 1], :] = jnp.zeros((STARTS[s + 1] - full, WIDTH), BF16)

    ids = clu[...].reshape(1, ROWS)
    n_clusters = omap.shape[0]
    which = onehot(iota((n_clusters, ROWS), 0) == ids)
    step = iota((N_OWN, n_clusters), 0)
    owner_of = jnp.zeros((N_OWN, n_clusters), jnp.int32)
    for j in range(N_OWN):
        owner_of = jnp.where(step == j, dest[j], owner_of)
    mine = dot(onehot(owner_of == omap[...].reshape(1, n_clusters)), which)
    own_mask[...] = mine
    part = 256
    before = onehot(iota((part, part), 0) < iota((part, part), 1))
    base = jnp.zeros((N_OWN, 1), F32)
    pieces = []
    for i in range(ROWS // part):
        piece = mine[:, i * part:(i + 1) * part]
        pieces.append(dot(piece.astype(BF16), before) + base)
        base = base + jnp.sum(piece, axis=1, keepdims=True)
    rank = jnp.sum(mine * jnp.concatenate(pieces, axis=1), axis=0, keepdims=True)
    slot = jnp.sum(mine * iota((N_OWN, ROWS), 0).astype(F32), axis=0, keepdims=True) * SHARE + rank
    slot = slot.astype(jnp.int32)
    at_rank = onehot(iota((128, ROWS), 0) == rank.astype(jnp.int32))
    onehot_rank[...] = at_rank
    labels = dot_t((mine * ids.astype(F32)).astype(BF16), at_rank)
    for j in range(N_OWN):
        msend[j] = labels[j:j + 1, :]
    meta[0, 0] = msend[0]

    pl.semaphore_wait(barrier, len(peers))

    meta_out = []
    for j in range(1, N_OWN):
        meta_out.append(copy(msend.at[j], meta.at[0, j], m_s.at[j], m_r.at[j], (dest[j], t)))
        meta_out[-1].start()

    along, across = {}, {}
    out_copies = {}

    def pass_across(j):
        across[j] = copy(held.at[0, place(j)], held.at[1, place(j)], f_s.at[1, j], f_r.at[1, j], sib)
        across[j].start()

    def pass_along(j):
        if j >= LAG:
            for cp in along[j - LAG]:
                cp.wait_send()
        along[j] = [
            copy(held.at[0, place(j)], held.at[b, place(j)], f_s.at[b, j], f_r.at[b, j], device)
            for b, device in ((2, above), (3, below))
        ]
        for cp in along[j]:
            cp.start()

    def prepare(g):
        lo, hi = GROUPS[g]
        take = onehot(iota(((hi - lo) * SHARE, ROWS), 0) + lo * SHARE == slot)
        outbox[block(lo, hi - lo), :] = dot(take, unit[...]).astype(BF16)
        if lo == 0:
            held[0, place(0), :] = outbox[block(0), :]
            pass_across(0)

    def send(g):
        for j in range(max(GROUPS[g][0], 1), GROUPS[g][1]):
            out_copies[j] = copy(
                outbox.at[block(j)], held.at[0, place(j)], a_s.at[j], a_r.at[j], (dest[j], t)
            )
            out_copies[j].start()

    def receive(j):
        out_copies[j].wait_recv()
        pass_across(j)

    position = iota((1, TALL), 1)
    lane_j = jnp.full((1, TALL), -1, jnp.int32)
    lane_k = jnp.full((1, TALL), -1, jnp.int32)
    lane_key = jnp.zeros((1, TALL), jnp.int32)
    for j in range(N_OWN):
        inside = (position >= PLACE[j]) & (position < PLACE[j] + SHARE)
        lane_j = jnp.where(inside, j, lane_j)
        lane_k = jnp.where(inside, position - PLACE[j], lane_k)
        lane_key = jnp.where(inside, origin[j] * 1024 + position - PLACE[j], lane_key)
    lane_key = lane_key.astype(F32)
    tile_of = [t, 2 * y + (1 - k), 2 * down + k, 2 * up + k, 2 * up + (1 - k)]
    spread = onehot(iota((128, TALL), 0) == lane_k)
    in_block = onehot(iota((N_OWN, TALL), 0) == lane_j).astype(F32)

    for b in range(5):
        rowacc[b] = jnp.full((TALL, 128), -1.0, F32)
        lanebest[b] = jnp.full((1, TALL), -1.0, F32)

    meta_fwd = []

    def pass_labels():
        for cp in meta_out:
            cp.wait()
        for b, device in ((1, sib), (2, above), (3, below), (4, below_x)):
            meta_fwd.append(copy(meta.at[0], meta.at[b], g_s.at[b], g_r.at[b], device))
            meta_fwd[-1].start()

    def take_labels():
        for cp in meta_fwd:
            cp.wait()
        for b in range(5):
            lane = jnp.sum(
                in_block * dot(meta[b, :, 0, :].astype(BF16), spread), axis=0, keepdims=True
            )
            lane = jnp.where(lane_j >= 0, lane, F32(-1.0))
            key = lane_key + (tile_of[b] * 128).astype(F32)
            lane_clu[b] = lane
            lane_keys[b] = key
            col_info[b] = jnp.where(iota((128, TALL), 0) == 0, lane, key).T

    second = {}

    def compare(a, b, s, rows):
        width = STARTS[s + 1] - STARTS[s]
        new = pl.ds(STARTS[s], width)
        col_clu = lane_clu[a, :, new]
        col_key = lane_keys[a, :, new]
        best = lanebest[a, :, new]
        for top in range(0, rows, STRIP):
            strip = pl.ds(top, min(STRIP, rows - top))
            scores = dot_t(held[b, strip, :], held[a, new, :])
            same = jnp.where(col_info[b, strip, 0:1] == col_clu, scores, F32(-1.0))
            row_key = col_info[b, strip, 1:2]
            as_row = jnp.where(row_key > col_key, same, F32(-1.0))
            as_col = jnp.where(row_key < col_key, same, F32(-1.0))
            best = jnp.maximum(best, jnp.max(as_col, axis=0, keepdims=True))
            part = rowacc[b, strip, :]
            for i in range(0, width, 128):
                part = jnp.maximum(part, as_row[:, i:i + 128])
            rowacc[b, strip, :] = part
        lanebest[a, :, new] = best

    def inner(s):
        for j in range(*STAGES[s]):
            across[j].wait_recv()
        for b in (0, 1):
            compare(0, b, s, STARTS[s + 1])

    def arrive(s):
        for j in range(*STAGES[s]):
            for cp in along[j]:
                cp.wait_recv()
            second[j] = copy(held.at[3, place(j)], held.at[4, place(j)], s_s.at[j], s_r.at[j], sib)
            second[j].start()

    def with_owners(s):
        compare(3, 0, s, TALL)
        compare(3, 1, s, TALL)

    def with_above(s):
        compare(2, 3, s, STARTS[s + 1])

    def with_far(s):
        for j in range(*STAGES[s]):
            second[j].wait_recv()
        compare(2, 4, s, STARTS[s + 1])

    for action in ORDER:
        what, i = action[0], int(action[1:] or 0)
        if what == "P":
            prepare(i)
        elif what == "S":
            send(i)
        elif what == "W":
            receive(i)
        elif what == "F":
            pass_along(i)
        elif what == "L":
            pass_labels()
        elif what == "M":
            take_labels()
        elif what == "O":
            inner(i)
        elif what == "U":
            with_owners(i)
        elif what == "A":
            arrive(i)
        elif what == "D":
            with_above(i)
        else:
            with_far(i)

    for b in range(5):
        best = lanebest[b]
        if b != 2:
            best = jnp.maximum(best, jnp.max(rowacc[b].T, axis=0, keepdims=True))
        resend[b] = best
    back = [
        copy(resend.at[b], reget.at[b - 1], q_s.at[b], q_r.at[b], device)
        for b, device in ((1, sib), (2, below), (3, above), (4, above_x))
    ]
    for cp in back:
        cp.start()
    for cp in back:
        cp.wait_recv()
    total = resend[0]
    for b in range(4):
        total = jnp.maximum(total, reget[b])
    parts = dot_t(split3(in_block * total), spread)
    parts = parts[:N_OWN] + parts[N_OWN:2 * N_OWN] + parts[2 * N_OWN:]
    for j in range(N_OWN):
        retsend[j] = parts[j:j + 1, :]
    retget[0] = retsend[0]
    returns = [
        copy(retsend.at[j], retget.at[j], t_s.at[j], t_r.at[j], (origin[j], t))
        for j in range(1, N_OWN)
    ]
    for cp in returns:
        cp.start()
    for cp in returns:
        cp.wait_recv()
    values = dot(split3(retget[:, 0, :]), onehot_rank[...])
    values = values[:N_OWN] + values[N_OWN:2 * N_OWN] + values[2 * N_OWN:]
    out[...] = jnp.sum(values * own_mask[...], axis=0)

    left = [cp for j in range(N_OWN - LAG, N_OWN) for cp in along[j]]
    for cp in [*out_copies.values(), *across.values(), *second.values(), *left, *back, *returns]:
        cp.wait_send()


def on_device(embeddings, cluster, owner_map):
    dma = pltpu.SemaphoreType.DMA
    scratch = [
        pltpu.VMEM((ROWS, WIDTH), BF16),
        pltpu.VMEM((ROWS, WIDTH), BF16),
        pltpu.VMEM((ROWS, WIDTH), BF16),
        pltpu.VMEM((5, TALL, WIDTH), BF16),
        pltpu.VMEM((N_OWN, 1, 128), F32),
        pltpu.VMEM((5, N_OWN, 1, 128), F32),
        pltpu.VMEM((128, ROWS), BF16),
        pltpu.VMEM((N_OWN, ROWS), F32),
        pltpu.VMEM((5, 1, TALL), F32),
        pltpu.VMEM((5, 1, TALL), F32),
        pltpu.VMEM((5, TALL, 128), F32),
        pltpu.VMEM((5, TALL, 128), F32),
        pltpu.VMEM((5, 1, TALL), F32),
        pltpu.VMEM((5, 1, TALL), F32),
        pltpu.VMEM((4, 1, TALL), F32),
        pltpu.VMEM((N_OWN, 1, 128), F32),
        pltpu.VMEM((N_OWN, 1, 128), F32),
        dma((N_OWN,)), dma((N_OWN,)),
        dma((N_OWN,)), dma((N_OWN,)),
        dma((4, N_OWN)), dma((4, N_OWN)),
        dma((5,)), dma((5,)),
        dma((N_OWN,)), dma((N_OWN,)),
        dma((5,)), dma((5,)),
        dma((N_OWN,)), dma((N_OWN,)),
        dma,
    ]
    vmem = pl.BlockSpec(memory_space=pltpu.VMEM)
    best = pl.pallas_call(
        kernel,
        out_shape=jax.ShapeDtypeStruct((ROWS,), F32),
        in_specs=[pl.BlockSpec(memory_space=pl.ANY), vmem, vmem],
        out_specs=vmem,
        scratch_shapes=scratch,
        compiler_params=pltpu.CompilerParams(
            collective_id=0, has_side_effects=True, vmem_limit_bytes=56 << 20
        ),
    )(embeddings, cluster, owner_map)
    return best


def solution(mesh):
    placed = (P(("clu", "tile"), None), P(("clu", "tile")), P())
    return jax.shard_map(
        on_device, mesh=mesh, in_specs=placed, out_specs=P(("clu", "tile")), check_vma=False
    )
```

```python
import functools

import jax
import jax.numpy as jnp
from jax import lax
from jax.experimental import pallas as pl
from jax.experimental.pallas import tpu as pltpu
from jax.sharding import PartitionSpec as P

MESH = pl.DeviceIdType.MESH
F32 = jnp.float32
BF16 = jnp.bfloat16

SIDE = 4
OFFS = [
    (0, 0),
    (0, 1), (1, 0), (0, 3), (3, 0),
    (1, 1), (3, 3), (1, 3), (3, 1),
    (0, 2), (2, 0), (1, 2), (2, 1),
    (3, 2), (2, 3), (2, 2),
]
N_OWN = len(OFFS)
ROWS = 1280
SHARE = ROWS // N_OWN
WIDTH = 768
GROUPS = [(0, 5), (5, 9), (9, 13), (13, 16)]
STAGES = [(0, 4), (4, 7), (7, 10), (10, 13), (13, 16)]
STRIP = 352
LAG = 3
ORDER = [
    "F0", "P0", "S0", "N", "P1", "S1", "I", "P2", "W1", "F1", "W2", "F2", "S2", "L", "P3", "W3",
    "F3", "W4", "F4", "S3", "W5", "F5", "M", "O0", "W6", "W7", "F6", "O1", "W8", "F7", "A0",
    "D0", "W9", "F8", "X0", "W10", "W11", "F9", "O2", "W12", "F10", "A1", "D1", "W13", "F11",
    "X1", "W14", "W15", "F12", "O3", "O4", "F13", "A2", "D2", "U0", "F14", "X2", "U1", "U2",
    "F15", "A3", "U3", "D3", "X3", "A4", "U4", "D4", "X4",
]


def align(n, m):
    return -(-n // m) * m


STARTS = [0]
for lo, hi in STAGES:
    STARTS.append(STARTS[-1] + align((hi - lo) * SHARE, 128))
TALL = STARTS[-1]
PLACE = [STARTS[s] + (j - lo) * SHARE for s, (lo, hi) in enumerate(STAGES) for j in range(lo, hi)]


def dot_t(a, b):
    return lax.dot_general(a, b, (((1,), (1,)), ((), ())), preferred_element_type=F32)


def dot(a, b):
    return jnp.dot(a, b, preferred_element_type=F32)


def split3(v):
    hi = v.astype(BF16)
    rest = v - hi.astype(F32)
    mid = rest.astype(BF16)
    low = (rest - mid.astype(F32)).astype(BF16)
    return jnp.concatenate([hi, mid, low], axis=0)


def iota(shape, dim):
    return lax.broadcasted_iota(jnp.int32, shape, dim)


def onehot(mask):
    return jnp.where(mask, F32(1.0), F32(0.0)).astype(BF16)


def kernel(
    emb_hbm, clu, omap, out,
    emb, unit, outbox, held, msend, meta, onehot_rank, own_mask,
    lane_clu, lane_keys, col_info, rowacc, lanebest, resend, reget, retsend, retget,
    a_s, a_r, m_s, m_r, f_s, f_r, g_s, g_r, s_s, s_r, q_s, q_r, t_s, t_r, e_s,
):
    c = lax.axis_index("clu")
    t = lax.axis_index("tile")
    x, z, y, k = c // SIDE, c % SIDE, t // 2, t % 2

    def shifted(dx, dz):
        return ((x + dx) % SIDE) * SIDE + (z + dz) % SIDE

    dest = [shifted(dx, dz) for dx, dz in OFFS]
    origin = [shifted(SIDE - dx, SIDE - dz) for dx, dz in OFFS]
    up, down = (y + 1) % SIDE, (y + SIDE - 1) % SIDE
    sib = (c, 2 * y + (1 - k))
    above, below = (c, 2 * up + k), (c, 2 * down + k)
    above_x, below_x = (c, 2 * up + (1 - k)), (c, 2 * down + (1 - k))

    load = pltpu.make_async_copy(emb_hbm, emb, e_s)
    load.start()
    barrier = pltpu.get_barrier_semaphore()
    peers = [(d, t) for d in dest[1:]] + [sib, above, below, above_x, below_x]
    for peer in peers:
        pl.semaphore_signal(barrier, inc=1, device_id=peer, device_id_type=MESH)

    def copy(src, dst, ssem, rsem, device):
        return pltpu.make_async_remote_copy(
            src_ref=src, dst_ref=dst, send_sem=ssem, recv_sem=rsem,
            device_id=device, device_id_type=MESH,
        )

    def block(j, n=1):
        return pl.ds(j * SHARE, n * SHARE)

    def place(j):
        return pl.ds(PLACE[j], SHARE)

    load.wait()
    def normalise(i, carry):
        rows = pl.ds(i * SHARE, SHARE)
        v = emb[rows, :].astype(F32)
        unit[rows, :] = (v * lax.rsqrt(jnp.sum(v * v, axis=1, keepdims=True) + 1e-06)).astype(BF16)
        return carry

    lax.fori_loop(0, N_OWN, normalise, 0)

    for s, (lo, hi) in enumerate(STAGES):
        full = STARTS[s] + (hi - lo) * SHARE
        if STARTS[s + 1] > full:
            for b in range(5):
                held[b, full:STARTS[s + 1], :] = jnp.zeros((STARTS[s + 1] - full, WIDTH), BF16)

    ids = clu[...].reshape(1, ROWS)
    n_clusters = omap.shape[0]
    which = onehot(iota((n_clusters, ROWS), 0) == ids)
    step = iota((N_OWN, n_clusters), 0)
    owner_of = jnp.zeros((N_OWN, n_clusters), jnp.int32)
    for j in range(N_OWN):
        owner_of = jnp.where(step == j, dest[j], owner_of)
    mine = dot(onehot(owner_of == omap[...].reshape(1, n_clusters)), which)
    own_mask[...] = mine
    part = 256
    before = onehot(iota((part, part), 0) < iota((part, part), 1))
    base = jnp.zeros((N_OWN, 1), F32)
    pieces = []
    for i in range(ROWS // part):
        piece = mine[:, i * part:(i + 1) * part]
        pieces.append(dot(piece.astype(BF16), before) + base)
        base = base + jnp.sum(piece, axis=1, keepdims=True)
    rank = jnp.sum(mine * jnp.concatenate(pieces, axis=1), axis=0, keepdims=True)
    slot = jnp.sum(mine * iota((N_OWN, ROWS), 0).astype(F32), axis=0, keepdims=True) * SHARE + rank
    slot = slot.astype(jnp.int32)
    at_rank = onehot(iota((128, ROWS), 0) == rank.astype(jnp.int32))
    onehot_rank[...] = at_rank
    labels = dot_t((mine * ids.astype(F32)).astype(BF16), at_rank)
    for j in range(N_OWN):
        msend[j] = labels[j:j + 1, :]
    meta[0, 0] = msend[0]

    def sort_group(g):
        lo, hi = GROUPS[g]
        take = onehot(iota(((hi - lo) * SHARE, ROWS), 0) + lo * SHARE == slot)
        outbox[block(lo, hi - lo), :] = dot(take, unit[...]).astype(BF16)
        if lo == 0:
            held[0, place(0), :] = outbox[block(0), :]

    sort_group(0)
    pl.semaphore_wait(barrier, len(peers))

    along, across = {}, {}
    out_copies = {}

    def pass_across(j):
        across[j] = copy(held.at[0, place(j)], held.at[1, place(j)], f_s.at[1, j], f_r.at[1, j], sib)
        across[j].start()

    def pass_along(j):
        if j >= LAG:
            for cp in along[j - LAG]:
                cp.wait_send()
        along[j] = [
            copy(held.at[0, place(j)], held.at[b, place(j)], f_s.at[b, j], f_r.at[b, j], device)
            for b, device in ((2, above), (3, below))
        ]
        for cp in along[j]:
            cp.start()

    def prepare(g):
        if g == 0:
            pass_across(0)
        else:
            sort_group(g)

    def send(g):
        for j in range(max(GROUPS[g][0], 1), GROUPS[g][1]):
            out_copies[j] = copy(
                outbox.at[block(j)], held.at[0, place(j)], a_s.at[j], a_r.at[j], (dest[j], t)
            )
            out_copies[j].start()

    def receive(j):
        out_copies[j].wait_recv()
        pass_across(j)

    def find_places():
        position = iota((1, TALL), 1)
        lane_j = jnp.full((1, TALL), -1, jnp.int32)
        lane_k = jnp.full((1, TALL), -1, jnp.int32)
        lane_key = jnp.zeros((1, TALL), jnp.int32)
        for j in range(N_OWN):
            inside = (position >= PLACE[j]) & (position < PLACE[j] + SHARE)
            lane_j = jnp.where(inside, j, lane_j)
            lane_k = jnp.where(inside, position - PLACE[j], lane_k)
            lane_key = jnp.where(inside, origin[j] * 1024 + position - PLACE[j], lane_key)
        lane_key = lane_key.astype(F32)
        tile_of = [t, 2 * y + (1 - k), 2 * down + k, 2 * up + k, 2 * up + (1 - k)]
        spread = onehot(iota((128, TALL), 0) == lane_k)
        in_block = onehot(iota((N_OWN, TALL), 0) == lane_j).astype(F32)
        return lane_j, lane_key, tile_of, spread, in_block

    places = []

    def clear():
        for b in range(5):
            rowacc[b] = jnp.full((TALL, 128), -1.0, F32)
            lanebest[b] = jnp.full((1, TALL), -1.0, F32)

    meta_out = []

    def send_labels():
        for j in range(1, N_OWN):
            cp = copy(msend.at[j], meta.at[0, j], m_s.at[j], m_r.at[j], (dest[j], t))
            cp.start()
            meta_out.append(cp)

    meta_fwd = []

    def pass_labels():
        for cp in meta_out:
            cp.wait()
        for b, device in ((1, sib), (2, above), (3, below), (4, below_x)):
            meta_fwd.append(copy(meta.at[0], meta.at[b], g_s.at[b], g_r.at[b], device))
            meta_fwd[-1].start()

    def take_labels():
        lane_j, lane_key, tile_of, spread, in_block = places
        for cp in meta_fwd:
            cp.wait()
        for b in range(5):
            lane = jnp.sum(
                in_block * dot(meta[b, :, 0, :].astype(BF16), spread), axis=0, keepdims=True
            )
            lane = jnp.where(lane_j >= 0, lane, F32(-1.0))
            key = lane_key + (tile_of[b] * 128).astype(F32)
            lane_clu[b] = lane
            lane_keys[b] = key
            col_info[b] = jnp.where(iota((128, TALL), 0) == 0, lane, key).T

    second = {}

    def compare(a, b, s, rows):
        width = STARTS[s + 1] - STARTS[s]
        new = pl.ds(STARTS[s], width)
        col_clu = lane_clu[a, :, new]
        col_key = lane_keys[a, :, new]
        best = lanebest[a, :, new]
        for top in range(0, rows, STRIP):
            strip = pl.ds(top, min(STRIP, rows - top))
            scores = dot_t(held[b, strip, :], held[a, new, :])
            same = jnp.where(col_info[b, strip, 0:1] == col_clu, scores, F32(-1.0))
            row_key = col_info[b, strip, 1:2]
            as_row = jnp.where(row_key > col_key, same, F32(-1.0))
            as_col = jnp.where(row_key < col_key, same, F32(-1.0))
            best = jnp.maximum(best, jnp.max(as_col, axis=0, keepdims=True))
            part = rowacc[b, strip, :]
            for i in range(0, width, 128):
                part = jnp.maximum(part, as_row[:, i:i + 128])
            rowacc[b, strip, :] = part
        lanebest[a, :, new] = best

    def inner(s):
        for j in range(*STAGES[s]):
            across[j].wait_recv()
        for b in (0, 1):
            compare(0, b, s, STARTS[s + 1])

    def arrive(s):
        for j in range(*STAGES[s]):
            for cp in along[j]:
                cp.wait_recv()
            second[j] = copy(held.at[3, place(j)], held.at[4, place(j)], s_s.at[j], s_r.at[j], sib)
            second[j].start()

    def with_owners(s):
        compare(3, 0, s, TALL)
        compare(3, 1, s, TALL)

    def with_above(s):
        compare(2, 3, s, STARTS[s + 1])

    def with_far(s):
        for j in range(*STAGES[s]):
            second[j].wait_recv()
        compare(2, 4, s, STARTS[s + 1])

    for action in ORDER:
        what, i = action[0], int(action[1:] or 0)
        if what == "P":
            prepare(i)
        elif what == "S":
            send(i)
        elif what == "W":
            receive(i)
        elif what == "F":
            pass_along(i)
        elif what == "N":
            send_labels()
        elif what == "I":
            clear()
            places.extend(find_places())
        elif what == "L":
            pass_labels()
        elif what == "M":
            take_labels()
        elif what == "O":
            inner(i)
        elif what == "U":
            with_owners(i)
        elif what == "A":
            arrive(i)
        elif what == "D":
            with_above(i)
        else:
            with_far(i)

    spread, in_block = places[3:]
    for b in range(5):
        best = lanebest[b]
        if b != 2:
            best = jnp.maximum(best, jnp.max(rowacc[b].T, axis=0, keepdims=True))
        resend[b] = best
    back = [
        copy(resend.at[b], reget.at[b - 1], q_s.at[b], q_r.at[b], device)
        for b, device in ((1, sib), (2, below), (3, above), (4, above_x))
    ]
    for cp in back:
        cp.start()
    left = [cp for j in range(N_OWN - LAG, N_OWN) for cp in along[j]]
    for cp in [*out_copies.values(), *across.values(), *second.values(), *left]:
        cp.wait_send()
    for cp in back:
        cp.wait()
    total = resend[0]
    for b in range(4):
        total = jnp.maximum(total, reget[b])
    parts = dot_t(split3(in_block * total), spread)
    parts = parts[:N_OWN] + parts[N_OWN:2 * N_OWN] + parts[2 * N_OWN:]
    for j in range(N_OWN):
        retsend[j] = parts[j:j + 1, :]
    retget[0] = retsend[0]
    returns = [
        copy(retsend.at[j], retget.at[j], t_s.at[j], t_r.at[j], (origin[j], t))
        for j in reversed(range(1, N_OWN))
    ]
    for cp in returns:
        cp.start()
    for cp in returns:
        cp.wait_recv()
    values = dot(split3(retget[:, 0, :]), onehot_rank[...])
    values = values[:N_OWN] + values[N_OWN:2 * N_OWN] + values[2 * N_OWN:]
    out[...] = jnp.sum(values * own_mask[...], axis=0)

    for cp in returns:
        cp.wait_send()


def on_device(embeddings, cluster, owner_map):
    dma = pltpu.SemaphoreType.DMA
    scratch = [
        pltpu.VMEM((ROWS, WIDTH), BF16),
        pltpu.VMEM((ROWS, WIDTH), BF16),
        pltpu.VMEM((ROWS, WIDTH), BF16),
        pltpu.VMEM((5, TALL, WIDTH), BF16),
        pltpu.VMEM((N_OWN, 1, 128), F32),
        pltpu.VMEM((5, N_OWN, 1, 128), F32),
        pltpu.VMEM((128, ROWS), BF16),
        pltpu.VMEM((N_OWN, ROWS), F32),
        pltpu.VMEM((5, 1, TALL), F32),
        pltpu.VMEM((5, 1, TALL), F32),
        pltpu.VMEM((5, TALL, 128), F32),
        pltpu.VMEM((5, TALL, 128), F32),
        pltpu.VMEM((5, 1, TALL), F32),
        pltpu.VMEM((5, 1, TALL), F32),
        pltpu.VMEM((4, 1, TALL), F32),
        pltpu.VMEM((N_OWN, 1, 128), F32),
        pltpu.VMEM((N_OWN, 1, 128), F32),
        dma((N_OWN,)), dma((N_OWN,)),
        dma((N_OWN,)), dma((N_OWN,)),
        dma((4, N_OWN)), dma((4, N_OWN)),
        dma((5,)), dma((5,)),
        dma((N_OWN,)), dma((N_OWN,)),
        dma((5,)), dma((5,)),
        dma((N_OWN,)), dma((N_OWN,)),
        dma,
    ]
    vmem = pl.BlockSpec(memory_space=pltpu.VMEM)
    best = pl.pallas_call(
        kernel,
        out_shape=jax.ShapeDtypeStruct((ROWS,), F32),
        in_specs=[pl.BlockSpec(memory_space=pl.ANY), vmem, vmem],
        out_specs=vmem,
        scratch_shapes=scratch,
        compiler_params=pltpu.CompilerParams(
            collective_id=0, has_side_effects=True, vmem_limit_bytes=56 << 20
        ),
    )(embeddings, cluster, owner_map)
    return best


def solution(mesh):
    placed = (P(("clu", "tile"), None), P(("clu", "tile")), P())
    return jax.shard_map(
        on_device, mesh=mesh, in_specs=placed, out_specs=P(("clu", "tile")), check_vma=False
    )
```

```python
import functools

import jax
import jax.numpy as jnp
from jax import lax
from jax.experimental import pallas as pl
from jax.experimental.pallas import tpu as pltpu
from jax.sharding import PartitionSpec as P

MESH = pl.DeviceIdType.MESH
F32 = jnp.float32
BF16 = jnp.bfloat16

SIDE = 4
OFFS = [
    (0, 0),
    (0, 1), (1, 0), (0, 3), (3, 0),
    (1, 1), (3, 3), (1, 3), (3, 1),
    (0, 2), (2, 0), (1, 2), (2, 1),
    (3, 2), (2, 3), (2, 2),
]
N_OWN = len(OFFS)
ROWS = 1280
SHARE = ROWS // N_OWN
WIDTH = 768
GROUPS = [(0, 5), (5, 9), (9, 13), (13, 16)]
STAGES = [(0, 4), (4, 7), (7, 10), (10, 13), (13, 16)]
STRIP = 352
LAG = 4
ORDER = [
    "F0", "P0", "S0", "N", "P1", "S1", "I", "P2", "W1", "F1", "W2", "F2", "S2", "L", "P3", "W3",
    "F3", "W4", "F4", "S3", "W5", "F5", "M", "O0", "W6", "W7", "F6", "O1", "W8", "F7", "A0",
    "D0", "W9", "F8", "X0", "W10", "W11", "F9", "O2", "W12", "F10", "A1", "D1", "W13", "F11",
    "X1", "W14", "W15", "F12", "O3", "O4", "F13", "A2", "D2", "U0", "F14", "X2", "U1", "F15",
    "U2", "A3", "D3", "U3", "X3", "A4", "D4", "U4", "X4",
]


def align(n, m):
    return -(-n // m) * m


STARTS = [0]
for lo, hi in STAGES:
    STARTS.append(STARTS[-1] + align((hi - lo) * SHARE, 128))
TALL = STARTS[-1]
PLACE = [STARTS[s] + (j - lo) * SHARE for s, (lo, hi) in enumerate(STAGES) for j in range(lo, hi)]


def dot_t(a, b):
    return lax.dot_general(a, b, (((1,), (1,)), ((), ())), preferred_element_type=F32)


def dot(a, b):
    return jnp.dot(a, b, preferred_element_type=F32)


def split3(v):
    hi = v.astype(BF16)
    rest = v - hi.astype(F32)
    mid = rest.astype(BF16)
    low = (rest - mid.astype(F32)).astype(BF16)
    return jnp.concatenate([hi, mid, low], axis=0)


def iota(shape, dim):
    return lax.broadcasted_iota(jnp.int32, shape, dim)


def onehot(mask):
    return jnp.where(mask, F32(1.0), F32(0.0)).astype(BF16)


def kernel(
    emb_hbm, clu, omap, out,
    emb, unit, outbox, held, msend, meta, onehot_rank, own_mask,
    lane_clu, lane_keys, col_info, rowacc, lanebest, resend, reget, retsend, retget,
    a_s, a_r, m_s, m_r, f_s, f_r, g_s, g_r, s_s, s_r, q_s, q_r, t_s, t_r, e_s,
):
    c = lax.axis_index("clu")
    t = lax.axis_index("tile")
    x, z, y, k = c // SIDE, c % SIDE, t // 2, t % 2

    def shifted(dx, dz):
        return ((x + dx) % SIDE) * SIDE + (z + dz) % SIDE

    dest = [shifted(dx, dz) for dx, dz in OFFS]
    origin = [shifted(SIDE - dx, SIDE - dz) for dx, dz in OFFS]
    up, down = (y + 1) % SIDE, (y + SIDE - 1) % SIDE
    sib = (c, 2 * y + (1 - k))
    above, below = (c, 2 * up + k), (c, 2 * down + k)
    above_x, below_x = (c, 2 * up + (1 - k)), (c, 2 * down + (1 - k))

    load = pltpu.make_async_copy(emb_hbm, emb, e_s)
    load.start()
    barrier = pltpu.get_barrier_semaphore()
    peers = [(d, t) for d in dest[1:]] + [sib, above, below, above_x, below_x]
    for peer in peers:
        pl.semaphore_signal(barrier, inc=1, device_id=peer, device_id_type=MESH)

    def copy(src, dst, ssem, rsem, device):
        return pltpu.make_async_remote_copy(
            src_ref=src, dst_ref=dst, send_sem=ssem, recv_sem=rsem,
            device_id=device, device_id_type=MESH,
        )

    def block(j, n=1):
        return pl.ds(j * SHARE, n * SHARE)

    def place(j):
        return pl.ds(PLACE[j], SHARE)

    load.wait()
    def normalise(i, carry):
        rows = pl.ds(i * SHARE, SHARE)
        v = emb[rows, :].astype(F32)
        unit[rows, :] = (v * lax.rsqrt(jnp.sum(v * v, axis=1, keepdims=True) + 1e-06)).astype(BF16)
        return carry

    lax.fori_loop(0, N_OWN, normalise, 0)

    for s, (lo, hi) in enumerate(STAGES):
        full = STARTS[s] + (hi - lo) * SHARE
        if STARTS[s + 1] > full:
            for b in range(5):
                held[b, full:STARTS[s + 1], :] = jnp.zeros((STARTS[s + 1] - full, WIDTH), BF16)

    ids = clu[...].reshape(1, ROWS)
    n_clusters = omap.shape[0]
    which = onehot(iota((n_clusters, ROWS), 0) == ids)
    step = iota((N_OWN, n_clusters), 0)
    owner_of = jnp.zeros((N_OWN, n_clusters), jnp.int32)
    for j in range(N_OWN):
        owner_of = jnp.where(step == j, dest[j], owner_of)
    mine = dot(onehot(owner_of == omap[...].reshape(1, n_clusters)), which)
    own_mask[...] = mine
    part = 256
    before = onehot(iota((part, part), 0) < iota((part, part), 1))
    base = jnp.zeros((N_OWN, 1), F32)
    pieces = []
    for i in range(ROWS // part):
        piece = mine[:, i * part:(i + 1) * part]
        pieces.append(dot(piece.astype(BF16), before) + base)
        base = base + jnp.sum(piece, axis=1, keepdims=True)
    rank = jnp.sum(mine * jnp.concatenate(pieces, axis=1), axis=0, keepdims=True)
    slot = jnp.sum(mine * iota((N_OWN, ROWS), 0).astype(F32), axis=0, keepdims=True) * SHARE + rank
    slot = slot.astype(jnp.int32)
    at_rank = onehot(iota((128, ROWS), 0) == rank.astype(jnp.int32))
    onehot_rank[...] = at_rank
    labels = dot_t((mine * ids.astype(F32)).astype(BF16), at_rank)
    for j in range(N_OWN):
        msend[j] = labels[j:j + 1, :]
    meta[0, 0] = msend[0]

    def sort_group(g):
        lo, hi = GROUPS[g]
        take = onehot(iota(((hi - lo) * SHARE, ROWS), 0) + lo * SHARE == slot)
        outbox[block(lo, hi - lo), :] = dot(take, unit[...]).astype(BF16)
        if lo == 0:
            held[0, place(0), :] = outbox[block(0), :]

    sort_group(0)
    pl.semaphore_wait(barrier, len(peers))

    along, across = {}, {}
    out_copies = {}

    def pass_across(j):
        across[j] = copy(held.at[0, place(j)], held.at[1, place(j)], f_s.at[1, j], f_r.at[1, j], sib)
        across[j].start()

    def pass_along(j):
        if j >= LAG:
            for cp in along[j - LAG]:
                cp.wait_send()
        along[j] = [
            copy(held.at[0, place(j)], held.at[b, place(j)], f_s.at[b, j], f_r.at[b, j], device)
            for b, device in ((2, above), (3, below))
        ]
        for cp in along[j]:
            cp.start()

    def prepare(g):
        if g == 0:
            pass_across(0)
        else:
            sort_group(g)

    def send(g):
        for j in range(max(GROUPS[g][0], 1), GROUPS[g][1]):
            out_copies[j] = copy(
                outbox.at[block(j)], held.at[0, place(j)], a_s.at[j], a_r.at[j], (dest[j], t)
            )
            out_copies[j].start()

    def receive(j):
        out_copies[j].wait_recv()
        pass_across(j)

    def find_places():
        position = iota((1, TALL), 1)
        lane_j = jnp.full((1, TALL), -1, jnp.int32)
        lane_k = jnp.full((1, TALL), -1, jnp.int32)
        lane_key = jnp.zeros((1, TALL), jnp.int32)
        for j in range(N_OWN):
            inside = (position >= PLACE[j]) & (position < PLACE[j] + SHARE)
            lane_j = jnp.where(inside, j, lane_j)
            lane_k = jnp.where(inside, position - PLACE[j], lane_k)
            lane_key = jnp.where(inside, origin[j] * 1024 + position - PLACE[j], lane_key)
        lane_key = lane_key.astype(F32)
        tile_of = [t, 2 * y + (1 - k), 2 * down + k, 2 * up + k, 2 * up + (1 - k)]
        spread = onehot(iota((128, TALL), 0) == lane_k)
        in_block = onehot(iota((N_OWN, TALL), 0) == lane_j).astype(F32)
        return lane_j, lane_key, tile_of, spread, in_block

    places = []

    def clear():
        for b in range(5):
            rowacc[b] = jnp.full((TALL, 128), -1.0, F32)
            lanebest[b] = jnp.full((1, TALL), -1.0, F32)

    meta_out = []

    def send_labels():
        for j in range(1, N_OWN):
            cp = copy(msend.at[j], meta.at[0, j], m_s.at[j], m_r.at[j], (dest[j], t))
            cp.start()
            meta_out.append(cp)

    meta_fwd = []

    def pass_labels():
        for cp in meta_out:
            cp.wait()
        for b, device in ((1, sib), (2, above), (3, below), (4, below_x)):
            meta_fwd.append(copy(meta.at[0], meta.at[b], g_s.at[b], g_r.at[b], device))
            meta_fwd[-1].start()

    def take_labels():
        lane_j, lane_key, tile_of, spread, in_block = places
        for cp in meta_fwd:
            cp.wait()
        for b in range(5):
            lane = jnp.sum(
                in_block * dot(meta[b, :, 0, :].astype(BF16), spread), axis=0, keepdims=True
            )
            lane = jnp.where(lane_j >= 0, lane, F32(-1.0))
            key = lane_key + (tile_of[b] * 128).astype(F32)
            lane_clu[b] = lane
            lane_keys[b] = key
            col_info[b] = jnp.where(iota((128, TALL), 0) == 0, lane, key).T

    second = {}

    def compare(a, b, s, rows, first=0):
        width = STARTS[s + 1] - STARTS[s]
        new = pl.ds(STARTS[s], width)
        col_clu = lane_clu[a, :, new]
        col_key = lane_keys[a, :, new]
        best = lanebest[a, :, new]
        for top in range(first, rows, STRIP):
            strip = pl.ds(top, min(STRIP, rows - top))
            scores = dot_t(held[b, strip, :], held[a, new, :])
            same = jnp.where(col_info[b, strip, 0:1] == col_clu, scores, F32(-1.0))
            row_key = col_info[b, strip, 1:2]
            as_row = jnp.where(row_key > col_key, same, F32(-1.0))
            as_col = jnp.where(row_key < col_key, same, F32(-1.0))
            best = jnp.maximum(best, jnp.max(as_col, axis=0, keepdims=True))
            part = rowacc[b, strip, :]
            for i in range(0, width, 128):
                part = jnp.maximum(part, as_row[:, i:i + 128])
            rowacc[b, strip, :] = part
        lanebest[a, :, new] = best

    def inner(s):
        for j in range(*STAGES[s]):
            across[j].wait_recv()
        for b in (0, 1):
            compare(0, b, s, STARTS[s + 1])

    def arrive(s):
        for j in range(*STAGES[s]):
            for cp in along[j]:
                cp.wait_recv()
            second[j] = copy(held.at[3, place(j)], held.at[4, place(j)], s_s.at[j], s_r.at[j], sib)
            second[j].start()

    def with_owners(s):
        for b in (0, 1):
            compare(3, b, s, TALL, STARTS[s])
        for b in (0, 1):
            compare(2, b, s, TALL, STARTS[s + 1])

    def with_above(s):
        compare(2, 3, s, STARTS[s + 1])

    def with_far(s):
        for j in range(*STAGES[s]):
            second[j].wait_recv()
        compare(2, 4, s, STARTS[s + 1])

    for action in ORDER:
        what, i = action[0], int(action[1:] or 0)
        if what == "P":
            prepare(i)
        elif what == "S":
            send(i)
        elif what == "W":
            receive(i)
        elif what == "F":
            pass_along(i)
        elif what == "N":
            send_labels()
        elif what == "I":
            clear()
            places.extend(find_places())
        elif what == "L":
            pass_labels()
        elif what == "M":
            take_labels()
        elif what == "O":
            inner(i)
        elif what == "U":
            with_owners(i)
        elif what == "A":
            arrive(i)
        elif what == "D":
            with_above(i)
        else:
            with_far(i)

    spread, in_block = places[3:]
    for b in range(5):
        best = lanebest[b]
        if b != 2:
            best = jnp.maximum(best, jnp.max(rowacc[b].T, axis=0, keepdims=True))
        resend[b] = best
    back = [
        copy(resend.at[b], reget.at[b - 1], q_s.at[b], q_r.at[b], device)
        for b, device in ((1, sib), (2, below), (3, above), (4, above_x))
    ]
    for cp in back:
        cp.start()
    left = [cp for j in range(N_OWN - LAG, N_OWN) for cp in along[j]]
    for cp in [*out_copies.values(), *across.values(), *second.values(), *left]:
        cp.wait_send()
    for cp in back:
        cp.wait()
    total = resend[0]
    for b in range(4):
        total = jnp.maximum(total, reget[b])
    parts = dot_t(split3(in_block * total), spread)
    parts = parts[:N_OWN] + parts[N_OWN:2 * N_OWN] + parts[2 * N_OWN:]
    for j in range(N_OWN):
        retsend[j] = parts[j:j + 1, :]
    retget[0] = retsend[0]
    returns = [
        copy(retsend.at[j], retget.at[j], t_s.at[j], t_r.at[j], (origin[j], t))
        for j in reversed(range(1, N_OWN))
    ]
    for cp in returns:
        cp.start()
    for cp in returns:
        cp.wait_recv()
    values = dot(split3(retget[:, 0, :]), onehot_rank[...])
    values = values[:N_OWN] + values[N_OWN:2 * N_OWN] + values[2 * N_OWN:]
    out[...] = jnp.sum(values * own_mask[...], axis=0)

    for cp in returns:
        cp.wait_send()


def on_device(embeddings, cluster, owner_map):
    dma = pltpu.SemaphoreType.DMA
    scratch = [
        pltpu.VMEM((ROWS, WIDTH), BF16),
        pltpu.VMEM((ROWS, WIDTH), BF16),
        pltpu.VMEM((ROWS, WIDTH), BF16),
        pltpu.VMEM((5, TALL, WIDTH), BF16),
        pltpu.VMEM((N_OWN, 1, 128), F32),
        pltpu.VMEM((5, N_OWN, 1, 128), F32),
        pltpu.VMEM((128, ROWS), BF16),
        pltpu.VMEM((N_OWN, ROWS), F32),
        pltpu.VMEM((5, 1, TALL), F32),
        pltpu.VMEM((5, 1, TALL), F32),
        pltpu.VMEM((5, TALL, 128), F32),
        pltpu.VMEM((5, TALL, 128), F32),
        pltpu.VMEM((5, 1, TALL), F32),
        pltpu.VMEM((5, 1, TALL), F32),
        pltpu.VMEM((4, 1, TALL), F32),
        pltpu.VMEM((N_OWN, 1, 128), F32),
        pltpu.VMEM((N_OWN, 1, 128), F32),
        dma((N_OWN,)), dma((N_OWN,)),
        dma((N_OWN,)), dma((N_OWN,)),
        dma((4, N_OWN)), dma((4, N_OWN)),
        dma((5,)), dma((5,)),
        dma((N_OWN,)), dma((N_OWN,)),
        dma((5,)), dma((5,)),
        dma((N_OWN,)), dma((N_OWN,)),
        dma,
    ]
    vmem = pl.BlockSpec(memory_space=pltpu.VMEM)
    best = pl.pallas_call(
        kernel,
        out_shape=jax.ShapeDtypeStruct((ROWS,), F32),
        in_specs=[pl.BlockSpec(memory_space=pl.ANY), vmem, vmem],
        out_specs=vmem,
        scratch_shapes=scratch,
        compiler_params=pltpu.CompilerParams(
            collective_id=0, has_side_effects=True, vmem_limit_bytes=56 << 20
        ),
    )(embeddings, cluster, owner_map)
    return best


def solution(mesh):
    placed = (P(("clu", "tile"), None), P(("clu", "tile")), P())
    return jax.shard_map(
        on_device, mesh=mesh, in_specs=placed, out_specs=P(("clu", "tile")), check_vma=False
    )
```
